32 devices in a mesh: req: 8 (over z, x), head: 4 (over y, core).
Axes of the slice: x: 2, y: 2, z: 4, core: 2. Of those that a mesh axis runs over, the one named last changes fastest.
Arguments:
- queries: bfloat16 [8, 16, 2048], P('req', None, 'head'), may hold values from -6 to 6
- forget_logits: bfloat16 [8, 16, 2048], P('req', None, 'head'), may hold values from -8 to 8
- values: bfloat16 [8, 16, 2048], P('req', None, 'head'), may hold values from -6 to 6
- gate_input: bfloat16 [8, 16, 2048], P('req', None, 'head'), may hold values from -6 to 6
- init_states: float32 [8, 16, 128, 128], P('req', 'head'), may hold values from -4 to 4
- norm_gain: float32 [128], replicated, may hold values from 0.1 to 1.9
- out_weight: bfloat16 [2048, 2048], P('head'), may hold values from -0.125 to 0.125
- dealing: int32 [8], P('req'), may hold values from 0 to 7, as said below
- accepted: int32 [8], P('req'), may hold values from 0 to 16, as said below
Outputs:
- verified: bfloat16 [8, 16, 2048], P('req', None, 'head')
- new_states: float32 [8, 16, 128, 128], P('req', 'head')
The draws below stay inside these ranges and needn't reach their ends.
Inputs may be any that keep to these rules, and one draw needn't show every extreme that they name: `dealing`: each request appears in exactly one dealt slot. `accepted`: some request accepts all 16 draft tokens and some accepts none.
All inputs are finite; a program needn't handle non-finite values.
Results may differ from the reference program's by a relative error of at most 0.0049.
Values may be sent and summed in bfloat16 or wider, within the bound.
A program may use at most 64 MiB of HBM per device.

```python
import jax
import jax.numpy as jnp
from jax import lax

HEADS = 16
HEAD_DIM = 128
D = 2048
DRAFT = 16
REQS = 8


def draw_dealing(key, part):
    shuffled = jax.random.permutation(jax.random.fold_in(key, 11), REQS).astype(jnp.int32)
    middle = REQS // 2
    where_middle = jnp.argmax(shuffled == middle)
    first_entry = shuffled[0]
    shuffled = shuffled.at[where_middle].set(first_entry).at[0].set(middle)
    return shuffled.astype(jnp.int32)


def draw_accepted(key, part):
    first_key, second_key = jax.random.split(jax.random.fold_in(key, 7))
    counts = jax.random.randint(first_key, (REQS,), 0, DRAFT + 1)
    shuffled = jax.random.permutation(second_key, REQS)
    counts = counts.at[shuffled[0]].set(DRAFT).at[shuffled[1]].set(0)
    return counts.astype(jnp.int32)


def levels(key, dims, cuts, low, top_value):
    factor_of = 1.0
    for position, parts in cuts:
        heights = jax.random.uniform(jax.random.fold_in(jax.random.fold_in(key, 6), position), (parts,), jnp.float32, low / len(cuts), top_value / len(cuts))
        factor_of = factor_of * jnp.repeat(jnp.exp(heights), dims[position] // parts).reshape((-1,) + (1,) * (len(dims) - 1 - position))
    return factor_of


def noise(key, dims, width, bound, shards=(), kind=jnp.bfloat16):
    entries = jax.random.normal(key, dims, jnp.float32) * width
    if len(shards) > 0:
        entries = levels(key, dims, shards, -0.22, 0.18) * entries
    return jnp.clip(entries, min=-bound, max=bound).astype(kind)


def setup_inputs(seed: int = 0) -> dict:
    streams_of = jax.random.split(jax.random.key(seed), 10)
    return {
        "queries": noise(streams_of[0], (REQS, DRAFT, D), 1.0, 6.0, ((0, 8), (2, 4))),
        "forget_logits": noise(streams_of[1], (REQS, DRAFT, D), 2.0, 8.0, ((0, 8), (2, 4))),
        "values": noise(streams_of[2], (REQS, DRAFT, D), 1.0, 6.0, ((0, 8), (2, 4))),
        "gate_input": noise(streams_of[3], (REQS, DRAFT, D), 1.0, 6.0, ((0, 8), (2, 4))),
        "init_states": noise(streams_of[4], (REQS, HEADS, HEAD_DIM, HEAD_DIM), 0.5, 4.0, ((0, 8), (1, 4)), jnp.float32),
        "norm_gain": jnp.clip(1.0 + 0.18 * jax.random.normal(streams_of[5], (HEAD_DIM,), jnp.float32), 0.1, 1.9),
        "out_weight": noise(streams_of[6], (D, D), D ** -0.5, 0.125, ((0, 4),)),
        "dealing": draw_dealing(jax.random.fold_in(streams_of[9], 71), 0),
        "accepted": draw_accepted(jax.random.fold_in(streams_of[9], 71), 0),
    }


lower_bound = 0.8
norm_eps = 1e-05

def reference(queries, forget_logits, values, gate_input, init_states, norm_gain, out_weight, dealing, accepted):
    request_total = dealing.shape[0]
    inverse = jnp.zeros((request_total,), jnp.int32).at[dealing].set(jnp.arange(request_total, dtype=jnp.int32))
    tokens_q = queries[inverse]
    tokens_f = forget_logits[inverse]
    tokens_v = values[inverse]
    tokens_g = gate_input[inverse]

    def heads_of(tensor):
        return jnp.moveaxis(tensor.astype(jnp.float32).reshape(request_total, DRAFT, HEADS, HEAD_DIM), 1, 0)
    query_seq = heads_of(tokens_q)
    forget_seq = lower_bound + (1.0 - lower_bound) * jax.nn.sigmoid(heads_of(tokens_f))
    value_seq = heads_of(tokens_v)
    numbers = jnp.arange(1, DRAFT + 1, dtype=jnp.int32)

    def advance(state_pair, inputs):
        current, chosen = state_pair
        query_now, forget_now, value_now, number = inputs
        current = forget_now[..., None] * current + (1.0 - forget_now)[..., None] * value_now[..., None, :]
        chosen = jnp.where((accepted == number)[:, None, None, None], current, chosen)
        output = jnp.einsum('rhk,rhkv->rhv', query_now, current, precision=lax.Precision.HIGHEST)
        return ((current, chosen), output)
    (last_state, chosen), outputs = lax.scan(advance, (init_states, init_states), (query_seq, forget_seq, value_seq, numbers))
    outputs = jnp.moveaxis(outputs, 0, 1)
    meansq = lax.optimization_barrier(jnp.mean(outputs * outputs, axis=-1, keepdims=True))
    gate_heads = tokens_g.astype(jnp.float32).reshape(request_total, DRAFT, HEADS, HEAD_DIM)
    mixed_rows = (outputs * lax.rsqrt(meansq + norm_eps) * norm_gain * jax.nn.silu(gate_heads)).astype(jnp.bfloat16)
    mixed_rows = mixed_rows.reshape(request_total * DRAFT, HEADS * HEAD_DIM)
    verified = jnp.dot(mixed_rows, out_weight, preferred_element_type=jnp.float32).astype(jnp.bfloat16)
    verified = verified.reshape(request_total, DRAFT, HEADS * HEAD_DIM)
    return (verified, chosen)
```

```python
import functools

import jax
import jax.numpy as jnp
from jax import lax
from jax.experimental import pallas as pl
from jax.experimental.pallas import tpu as pltpu
from jax.sharding import PartitionSpec as P

lower_bound = 0.8
norm_eps = 1e-05
MESH = pl.DeviceIdType.MESH
CHUNKS = 2


def split(x):
    high = x.astype(jnp.bfloat16)
    return high, (x - high.astype(jnp.float32)).astype(jnp.bfloat16)


def mm(a, b, dims=((1,), (0,))):
    return lax.dot_general(a, b, (dims, ((), ())), preferred_element_type=jnp.float32)


def running_product(x):
    rows = lax.broadcasted_iota(jnp.int32, x.shape, 0)
    step = 1
    while step < x.shape[0]:
        x = x * jnp.where(rows >= step, pltpu.roll(x, step, 0), 1.0)
        step *= 2
    return x


def kernel(
    n_req,
    n_head,
    inner,
    q_hbm,
    f_hbm,
    v_hbm,
    g_hbm,
    s_hbm,
    gain_ref,
    w_hbm,
    dealing_ref,
    accepted_ref,
    out_ref,
    new_hbm,
    gath,
    deals,
    cross_out,
    cross_in,
    own,
    states,
    states_high,
    states_low,
    new_states,
    weight,
    keys,
    decay,
    total,
    part_out,
    part_in,
    load_sem,
    state_sem,
    weight_sem,
    store_sem,
    deal_send,
    deal_recv,
    line_send,
    line_recv,
    cross_send,
    cross_recv,
    part_send,
    part_recv,
):
    outer = n_req // inner
    chunks, _, draft, width = gath.shape[1:]
    heads, size = states.shape[0], states.shape[2]
    per = heads // chunks
    columns = out_ref.shape[2]
    me = lax.axis_index("req")
    mine = lax.axis_index("head")
    place = me // inner
    lane = lax.rem(me, inner)
    across = place * inner + (inner - 1 - lane)
    line = [(lax.rem(place + k, outer), lax.rem(place + outer - k, outer)) for k in range(1, outer)]
    ring = [lax.rem(mine + k, n_head) for k in range(1, n_head)]

    loads = []
    for c in range(chunks):
        for a, ref in enumerate((q_hbm, f_hbm, v_hbm, g_hbm)):
            loads.append(
                pltpu.make_async_copy(
                    ref.at[0, :, pl.ds(c * width, width)], gath.at[place, c, a], load_sem.at[c, a]
                )
            )
            loads[-1].start()
    state_copy = pltpu.make_async_copy(s_hbm.at[0], states, state_sem)
    state_copy.start()
    weight_copy = pltpu.make_async_copy(w_hbm, weight, weight_sem)
    weight_copy.start()

    barrier = pltpu.get_barrier_semaphore()
    count = 0
    for to, _ in line:
        pl.semaphore_signal(
            barrier, inc=1, device_id=(to * inner + lane, mine), device_id_type=MESH
        )
        count += 1
    if inner > 1:
        pl.semaphore_signal(barrier, inc=1, device_id=(across, mine), device_id_type=MESH)
        count += 1
    for to in ring:
        pl.semaphore_signal(barrier, inc=1, device_id=(me, to), device_id_type=MESH)
        count += 1
    deals[place] = jnp.full(deals.shape[1:], dealing_ref[0], jnp.int32)
    pl.semaphore_wait(barrier, count)

    def deal_copy(k, slot, to):
        return pltpu.make_async_remote_copy(
            src_ref=deals.at[slot],
            dst_ref=deals.at[slot],
            send_sem=deal_send.at[k],
            recv_sem=deal_recv.at[slot],
            device_id=(to * inner + lane, mine),
            device_id_type=MESH,
        )

    def line_copy(k, c, slot, to):
        return pltpu.make_async_remote_copy(
            src_ref=gath.at[slot, c],
            dst_ref=gath.at[slot, c],
            send_sem=line_send.at[k, c],
            recv_sem=line_recv.at[slot, c],
            device_id=(to * inner + lane, mine),
            device_id_type=MESH,
        )

    for k, (to, _) in enumerate(line):
        deal_copy(k, place, to).start()
    for c in range(chunks):
        for a in range(4):
            loads[c * 4 + a].wait()
        for k, (to, _) in enumerate(line):
            line_copy(k, c, place, to).start()

    state_copy.wait()
    for h in range(heads):
        states_high[h], states_low[h] = split(states[h])

    for k, (to, source) in enumerate(line):
        deal_copy(k, source, to).wait_recv()

    def mask_of(slot, target):
        hit = jnp.where(deals[slot] == target, 1.0, 0.0)
        hit = jnp.concatenate([hit] * (draft // 8), axis=0).astype(jnp.bfloat16)
        return jnp.concatenate([hit] * (width // 128), axis=1)

    masks_own = [mask_of(slot, me) for slot in range(outer)]
    masks_across = [mask_of(slot, across) for slot in range(outer)] if inner > 1 else None

    def pick(masks, c, a):
        acc = masks[0] * gath[0, c, a]
        for slot in range(1, outer):
            acc = acc + masks[slot] * gath[slot, c, a]
        return acc

    def cross_copy(c):
        return pltpu.make_async_remote_copy(
            src_ref=cross_out.at[c],
            dst_ref=cross_in.at[c],
            send_sem=cross_send.at[c],
            recv_sem=cross_recv.at[c],
            device_id=(across, mine),
            device_id_type=MESH,
        )

    def route(c):
        for k, (to, source) in enumerate(line):
            line_copy(k, c, source, to).wait_recv()
        if inner > 1:
            for a in range(4):
                cross_out[c, a] = pick(masks_across, c, a)
            cross_copy(c).start()
        for a in range(4):
            own[c, a] = pick(masks_own, c, a)

    row = lax.broadcasted_iota(jnp.int32, (draft, draft), 0)
    column = lax.broadcasted_iota(jnp.int32, (draft, draft), 1)
    causal = row >= column

    def mix(c):
        if inner > 1:
            cross_copy(c).wait_recv()
            q, f, v, g = (own[c, a] + cross_in[c, a] for a in range(4))
            own[c, 2] = v
        else:
            q, f, v, g = (own[c, a] for a in range(4))
        forget = lower_bound + (1.0 - lower_bound) * jax.nn.sigmoid(f.astype(jnp.float32))
        products = running_product(forget)
        scaled = q.astype(jnp.float32) * products
        key = (1.0 - forget) / products
        decay[c] = products
        keys[c] = key
        gate = g.astype(jnp.float32)
        gate = gate * jax.nn.sigmoid(gate)
        q_high, q_low = split(scaled)
        k_high, k_low = split(key)
        results = []
        for i in range(per):
            h = c * per + i
            s = slice(i * size, (i + 1) * size)
            qh, ql = q_high[:, s], q_low[:, s]
            kh, kl = k_high[:, s], k_low[:, s]
            both = jnp.concatenate([qh, ql], axis=0)
            nt = ((1,), (1,))
            scores = mm(both, kh, nt)
            scores = scores[:draft] + scores[draft:] + mm(qh, kl, nt)
            scores = jnp.where(causal, scores, 0.0)
            a_high, a_low = split(scores)
            carried = mm(both, states_high[h])
            carried = carried[:draft] + carried[draft:] + mm(qh, states_low[h])
            local = mm(jnp.concatenate([a_high, a_low], axis=0), v[:, s])
            o = carried + local[:draft] + local[draft:]
            meansq = jnp.mean(o * o, axis=-1, keepdims=True)
            results.append(o * lax.rsqrt(meansq + norm_eps) * gain_ref[...] * gate[:, s])
        mixed = jnp.concatenate(results, axis=1).astype(jnp.bfloat16)
        return mixed

    def project(c, mixed, last):
        rows = pl.ds(c * width, width)
        for j in range(n_head):
            part = mm(mixed, weight[rows, j * columns : (j + 1) * columns])
            if c > 0:
                part = part + total[j]
            total[j] = part
            if last:
                part_out[j] = part.astype(jnp.bfloat16)

    def store_copy(h):
        return pltpu.make_async_copy(new_states.at[h], new_hbm.at[0, h], store_sem.at[h])

    def advance(c):
        taken = accepted_ref[0]
        rows = lax.broadcasted_iota(jnp.int32, (draft, width), 0)
        last = jnp.sum(jnp.where(rows == taken - 1, decay[c], 0.0), axis=0, keepdims=True)
        last = jnp.where(taken == 0, 1.0, last)
        key = jnp.where(rows < taken, keys[c] * last, 0.0)
        k_high, k_low = split(key)
        both = jnp.concatenate([k_high, k_low], axis=0)
        v = own[c, 2]
        twice = jnp.concatenate([v, v], axis=0)
        for i in range(per):
            h = c * per + i
            s = slice(i * size, (i + 1) * size)
            fade = jnp.broadcast_to(last[:, s], (size, size)).T
            new_states[h] = fade * states[h] + mm(both[:, s], twice[:, s], ((0,), (0,)))
            store_copy(h).start()

    def part_copy(k, slot, to):
        return pltpu.make_async_remote_copy(
            src_ref=part_out.at[to],
            dst_ref=part_in.at[slot],
            send_sem=part_send.at[k],
            recv_sem=part_recv.at[slot],
            device_id=(me, to),
            device_id_type=MESH,
        )

    for c in range(chunks):
        route(c)
        if c > 0:
            advance(c - 1)
        mixed = mix(c)
        if c == 0:
            weight_copy.wait()
        project(c, mixed, c == chunks - 1)
    for k, to in enumerate(ring):
        part_copy(k, mine, to).start()
    advance(chunks - 1)
    result = total[mine]
    for k in range(n_head - 1):
        source = lax.rem(mine + n_head - 1 - k, n_head)
        part_copy(k, source, ring[k]).wait_recv()
        result = result + part_in[source].astype(jnp.float32)
    out_ref[0] = result.astype(jnp.bfloat16)

    for k, (to, _) in enumerate(line):
        deal_copy(k, place, to).wait_send()
        for c in range(chunks):
            line_copy(k, c, place, to).wait_send()
    if inner > 1:
        for c in range(chunks):
            cross_copy(c).wait_send()
    for k, to in enumerate(ring):
        part_copy(k, mine, to).wait_send()
    for h in range(heads):
        store_copy(h).wait()


def per_device(n_req, n_head, *args):
    queries, forget_logits, values, gate_input, states, gain, weight, dealing, accepted = args
    draft, features = queries.shape[1:]
    heads, size = states.shape[1:3]
    columns = weight.shape[1] // n_head
    inner = 2 if n_req % 2 == 0 else 1
    outer = n_req // inner
    chunks = CHUNKS if heads % CHUNKS == 0 else 1
    width = features // chunks
    bf16, f32 = jnp.bfloat16, jnp.float32
    anywhere = pl.BlockSpec(memory_space=pl.ANY)
    vmem = pl.BlockSpec(memory_space=pltpu.VMEM)
    smem = pl.BlockSpec(memory_space=pltpu.SMEM)
    dma = pltpu.SemaphoreType.DMA
    return pl.pallas_call(
        functools.partial(kernel, n_req, n_head, inner),
        out_shape=(
            jax.ShapeDtypeStruct((1, draft, columns), bf16),
            jax.ShapeDtypeStruct(states.shape, f32),
        ),
        in_specs=[anywhere] * 5 + [vmem, anywhere, smem, smem],
        out_specs=(vmem, anywhere),
        scratch_shapes=[
            pltpu.VMEM((outer, chunks, 4, draft, width), bf16),
            pltpu.VMEM((outer, 8, 128), jnp.int32),
            pltpu.VMEM((chunks, 4, draft, width), bf16),
            pltpu.VMEM((chunks, 4, draft, width), bf16),
            pltpu.VMEM((chunks, 4, draft, width), bf16),
            pltpu.VMEM((heads, size, size), f32),
            pltpu.VMEM((heads, size, size), bf16),
            pltpu.VMEM((heads, size, size), bf16),
            pltpu.VMEM((heads, size, size), f32),
            pltpu.VMEM(weight.shape, bf16),
            pltpu.VMEM((chunks, draft, width), f32),
            pltpu.VMEM((chunks, draft, width), f32),
            pltpu.VMEM((n_head, draft, columns), f32),
            pltpu.VMEM((n_head, draft, columns), bf16),
            pltpu.VMEM((n_head, draft, columns), bf16),
            dma((chunks, 4)),
            dma,
            dma,
            dma((heads,)),
            dma((outer,)),
            dma((outer,)),
            dma((outer, chunks)),
            dma((outer, chunks)),
            dma((chunks,)),
            dma((chunks,)),
            dma((n_head,)),
            dma((n_head,)),
        ],
        compiler_params=pltpu.CompilerParams(
            collective_id=0, has_side_effects=True, vmem_limit_bytes=48 * 1024 * 1024
        ),
    )(
        queries,
        forget_logits,
        values,
        gate_input,
        states,
        gain.reshape(1, -1),
        weight,
        dealing,
        accepted,
    )


def solution(mesh):
    placed = (
        P("req", None, "head"),
        P("req", None, "head"),
        P("req", None, "head"),
        P("req", None, "head"),
        P("req", "head", None, None),
        P(),
        P("head", None),
        P("req"),
        P("req"),
    )
    return jax.shard_map(
        functools.partial(per_device, mesh.shape["req"], mesh.shape["head"]),
        mesh=mesh,
        in_specs=placed,
        out_specs=(P("req", None, "head"), P("req", "head", None, None)),
        check_vma=False,
    )
```

```python
import functools

import jax
import jax.numpy as jnp
from jax import lax
from jax.experimental import pallas as pl
from jax.experimental.pallas import tpu as pltpu
from jax.sharding import PartitionSpec as P

lower_bound = 0.8
norm_eps = 1e-05
MESH = pl.DeviceIdType.MESH
CHUNKS = 4


def split(x):
    high = x.astype(jnp.bfloat16)
    return high, (x - high.astype(jnp.float32)).astype(jnp.bfloat16)


def mm(a, b, dims=((1,), (0,))):
    return lax.dot_general(a, b, (dims, ((), ())), preferred_element_type=jnp.float32)


def running_product(x):
    rows = lax.broadcasted_iota(jnp.int32, x.shape, 0)
    step = 1
    while step < x.shape[0]:
        x = x * jnp.where(rows >= step, pltpu.roll(x, step, 0), 1.0)
        step *= 2
    return x


def kernel(
    n_req,
    n_head,
    inner,
    direct,
    order,
    q_hbm,
    f_hbm,
    v_hbm,
    g_hbm,
    s_hbm,
    gain_hbm,
    w_hbm,
    dealing,
    accepted,
    out_ref,
    new_ref,
    raw,
    gath,
    chosen,
    deals,
    cross_out,
    cross_in,
    own,
    states,
    states_high,
    states_low,
    weight,
    gain,
    keys,
    decay,
    total,
    part_out,
    part_in,
    load_sem,
    small_sem,
    deal_send,
    deal_recv,
    line_send,
    line_recv,
    cross_send,
    cross_recv,
    part_send,
    part_recv,
):
    outer = n_req // inner
    chunks, _, draft, width = raw.shape
    heads, size = states.shape[0], states.shape[2]
    per = heads // chunks
    columns = out_ref.shape[2]
    me = lax.axis_index("req")
    mine = lax.axis_index("head")
    place = me // inner
    lane = lax.rem(me, inner)
    across = place * inner + (inner - 1 - lane)
    line = [(lax.rem(place + k, outer), lax.rem(place + outer - k, outer)) for k in range(1, outer)]
    ring = [lax.rem(mine + k, n_head) for k in range(1, n_head)]

    def start(source, target, sem):
        copy = pltpu.make_async_copy(source, target, sem)
        copy.start()
        return copy

    loads = [None] * chunks
    for c in order:
        loads[c] = [
            start(ref.at[0, :, pl.ds(c * width, width)], raw.at[c, a], load_sem.at[c, a])
            for a, ref in enumerate((q_hbm, f_hbm, v_hbm, g_hbm))
        ]
    barrier = pltpu.get_barrier_semaphore()
    peers = [(to * inner + lane, mine) for to, _ in line]
    if inner > 1:
        peers.append((across, mine))
    peers += [(me, to) for to in ring]
    for peer in peers:
        pl.semaphore_signal(barrier, inc=1, device_id=peer, device_id_type=MESH)
    state_load = start(s_hbm.at[0], states, small_sem.at[0])
    weight_load = start(w_hbm, weight, small_sem.at[1])
    gain_load = start(gain_hbm, gain, small_sem.at[2])
    deals[place] = jnp.full(deals.shape[1:], dealing[0], jnp.int32)
    for c in order:
        for load in loads[c]:
            load.wait()
    pl.semaphore_wait(barrier, len(peers))

    def deal_copy(k, slot, to):
        return pltpu.make_async_remote_copy(
            src_ref=deals.at[place],
            dst_ref=deals.at[slot],
            send_sem=deal_send.at[k],
            recv_sem=deal_recv.at[slot],
            device_id=(to, mine),
            device_id_type=MESH,
        )

    def line_copy(k, c, slot, to):
        return pltpu.make_async_remote_copy(
            src_ref=raw.at[c] if c in direct else chosen.at[to, c],
            dst_ref=gath.at[slot, c],
            send_sem=line_send.at[k, c],
            recv_sem=line_recv.at[slot, c],
            device_id=(to * inner + lane, mine),
            device_id_type=MESH,
        )

    def cross_copy(c):
        return pltpu.make_async_remote_copy(
            src_ref=cross_out.at[c] if c in direct else raw.at[c],
            dst_ref=cross_in.at[c],
            send_sem=cross_send.at[c],
            recv_sem=cross_recv.at[c],
            device_id=(across, mine),
            device_id_type=MESH,
        )

    turned = [c for c in order if c not in direct]
    if inner > 1:
        deal_copy(outer - 1, outer, across).start()
    for k, (to, _) in enumerate(line):
        deal_copy(k, place, to * inner + lane).start()
    for c in turned:
        cross_copy(c).start()
    for c in direct:
        for k, (to, _) in enumerate(line):
            line_copy(k, c, place, to).start()

    def mask_of(slot, target):
        hit = jnp.where(deals[slot] == target, 1.0, 0.0)
        hit = jnp.concatenate([hit] * (draft // 8), axis=0).astype(jnp.bfloat16)
        return jnp.concatenate([hit] * (width // 128), axis=1)

    if turned:
        deal_copy(outer - 1, outer, across).wait_recv()
        first = [mask_of(place, slot * inner + lane) for slot in range(outer)]
        second = [mask_of(outer, slot * inner + lane) for slot in range(outer)]
        for c in turned:
            cross_copy(c).wait_recv()
            for slot in range(outer):
                for a in range(4):
                    chosen[slot, c, a] = first[slot] * raw[c, a] + second[slot] * cross_in[c, a]
            for k, (to, _) in enumerate(line):
                line_copy(k, c, place, to).start()

    state_load.wait()
    for h in range(heads):
        states_high[h], states_low[h] = split(states[h])

    for k, (to, source) in enumerate(line):
        deal_copy(k, source, to * inner + lane).wait_recv()

    def pick(target, c):
        masks = [mask_of(lax.rem(place + k, outer), target) for k in range(outer)]
        for a in range(4):
            acc = masks[0] * raw[c, a]
            for k in range(1, outer):
                acc = acc + masks[k] * gath[lax.rem(place + k, outer), c, a]
            yield a, acc

    def collect(c):
        for k, (to, source) in enumerate(line):
            line_copy(k, c, source, to).wait_recv()

    for c in direct:
        collect(c)
        if inner > 1:
            for a, tokens in pick(across, c):
                cross_out[c, a] = tokens
            cross_copy(c).start()
        for a, tokens in pick(me, c):
            own[c, a] = tokens

    def tokens_of(c):
        if c in direct:
            if inner == 1:
                return [own[c, a] for a in range(4)]
            cross_copy(c).wait_recv()
            return [own[c, a] + cross_in[c, a] for a in range(4)]
        collect(c)
        found = []
        for a in range(4):
            acc = chosen[place, c, a]
            for k in range(1, outer):
                acc = acc + gath[lax.rem(place + k, outer), c, a]
            found.append(acc)
        return found

    row = lax.broadcasted_iota(jnp.int32, (draft, draft), 0)
    column = lax.broadcasted_iota(jnp.int32, (draft, draft), 1)
    causal = row >= column

    def mix(c):
        q, f, v, g = tokens_of(c)
        own[c, 2] = v
        forget = lower_bound + (1.0 - lower_bound) * jax.nn.sigmoid(f.astype(jnp.float32))
        products = running_product(forget)
        scaled = q.astype(jnp.float32) * products
        key = (1.0 - forget) / products
        decay[c] = products
        keys[c] = key
        gate = g.astype(jnp.float32)
        gate = gate * jax.nn.sigmoid(gate)
        q_high, q_low = split(scaled)
        k_high, k_low = split(key)
        results = []
        for i in range(per):
            h = c * per + i
            s = slice(i * size, (i + 1) * size)
            qh, ql = q_high[:, s], q_low[:, s]
            kh, kl = k_high[:, s], k_low[:, s]
            both = jnp.concatenate([qh, ql], axis=0)
            nt = ((1,), (1,))
            scores = mm(both, kh, nt)
            scores = scores[:draft] + scores[draft:] + mm(qh, kl, nt)
            scores = jnp.where(causal, scores, 0.0)
            a_high, a_low = split(scores)
            carried = mm(both, states_high[h])
            carried = carried[:draft] + carried[draft:] + mm(qh, states_low[h])
            local = mm(jnp.concatenate([a_high, a_low], axis=0), v[:, s])
            o = carried + local[:draft] + local[draft:]
            meansq = jnp.mean(o * o, axis=-1, keepdims=True)
            results.append(o * lax.rsqrt(meansq + norm_eps) * gain[...] * gate[:, s])
        return jnp.concatenate(results, axis=1).astype(jnp.bfloat16)

    def project(c, mixed):
        rows = pl.ds(c * width, width)
        for j in range(n_head):
            part = mm(mixed, weight[rows, j * columns : (j + 1) * columns])
            if c != order[0]:
                part = part + total[j]
            total[j] = part
            if c == order[-1]:
                part_out[j] = part.astype(jnp.bfloat16)

    def advance(c):
        taken = accepted[0]
        rows = lax.broadcasted_iota(jnp.int32, (draft, width), 0)
        last = jnp.sum(jnp.where(rows == taken - 1, decay[c], 0.0), axis=0, keepdims=True)
        last = jnp.where(taken == 0, 1.0, last)
        key = jnp.where(rows < taken, keys[c] * last, 0.0)
        k_high, k_low = split(key)
        both = jnp.concatenate([k_high, k_low], axis=0)
        v = own[c, 2]
        twice = jnp.concatenate([v, v], axis=0)
        for i in range(per):
            h = c * per + i
            s = slice(i * size, (i + 1) * size)
            fade = jnp.broadcast_to(last[:, s], (size, size)).T
            new_ref[0, h] = fade * states[h] + mm(both[:, s], twice[:, s], ((0,), (0,)))

    def part_copy(k, slot, to):
        return pltpu.make_async_remote_copy(
            src_ref=part_out.at[to],
            dst_ref=part_in.at[slot],
            send_sem=part_send.at[k],
            recv_sem=part_recv.at[slot],
            device_id=(me, to),
            device_id_type=MESH,
        )

    gain_load.wait()
    weight_load.wait()
    for c in order:
        project(c, mix(c))
    for k, to in enumerate(ring):
        part_copy(k, mine, to).start()
    for c in order:
        advance(c)
    result = total[mine]
    for k in range(n_head - 1):
        source = lax.rem(mine + n_head - 1 - k, n_head)
        part_copy(k, source, ring[k]).wait_recv()
        result = result + part_in[source].astype(jnp.float32)
    out_ref[0] = result.astype(jnp.bfloat16)

    if inner > 1:
        deal_copy(outer - 1, outer, across).wait_send()
    for k, (to, _) in enumerate(line):
        deal_copy(k, place, to * inner + lane).wait_send()
        for c in range(chunks):
            line_copy(k, c, place, to).wait_send()
    if inner > 1:
        for c in range(chunks):
            cross_copy(c).wait_send()
    for k, to in enumerate(ring):
        part_copy(k, mine, to).wait_send()


def per_device(n_req, n_head, *args):
    queries, forget_logits, values, gate_input, states, gain, weight, dealing, accepted = args
    draft, features = queries.shape[1:]
    heads, size = states.shape[1:3]
    columns = weight.shape[1] // n_head
    inner = 2 if n_req % 2 == 0 else 1
    outer = n_req // inner
    chunks = CHUNKS if heads % CHUNKS == 0 else 1
    direct = (0,) if inner > 1 else tuple(range(chunks))
    order = (1, 0, 2, 3) if chunks == 4 else tuple(range(chunks))
    width = features // chunks
    bf16, f32 = jnp.bfloat16, jnp.float32
    hbm = pl.BlockSpec(memory_space=pltpu.HBM)
    vmem = pl.BlockSpec(memory_space=pltpu.VMEM)
    smem = pl.BlockSpec(memory_space=pltpu.SMEM)
    dma = pltpu.SemaphoreType.DMA
    return pl.pallas_call(
        functools.partial(kernel, n_req, n_head, inner, direct, order),
        out_shape=(
            jax.ShapeDtypeStruct((1, draft, columns), bf16),
            jax.ShapeDtypeStruct(states.shape, f32),
        ),
        in_specs=[hbm] * 7 + [smem] * 2,
        out_specs=(vmem, vmem),
        scratch_shapes=[
            pltpu.VMEM((chunks, 4, draft, width), bf16),
            pltpu.VMEM((outer, chunks, 4, draft, width), bf16),
            pltpu.VMEM((outer, chunks, 4, draft, width), bf16),
            pltpu.VMEM((outer + 1, 8, 128), jnp.int32),
            pltpu.VMEM((chunks, 4, draft, width), bf16),
            pltpu.VMEM((chunks, 4, draft, width), bf16),
            pltpu.VMEM((chunks, 4, draft, width), bf16),
            pltpu.VMEM((heads, size, size), f32),
            pltpu.VMEM((heads, size, size), bf16),
            pltpu.VMEM((heads, size, size), bf16),
            pltpu.VMEM(weight.shape, bf16),
            pltpu.VMEM((1, size), f32),
            pltpu.VMEM((chunks, draft, width), f32),
            pltpu.VMEM((chunks, draft, width), f32),
            pltpu.VMEM((n_head, draft, columns), f32),
            pltpu.VMEM((n_head, draft, columns), bf16),
            pltpu.VMEM((n_head, draft, columns), bf16),
            dma((chunks, 4)),
            dma((3,)),
            dma((outer,)),
            dma((outer + 1,)),
            dma((outer, chunks)),
            dma((outer, chunks)),
            dma((chunks,)),
            dma((chunks,)),
            dma((n_head,)),
            dma((n_head,)),
        ],
        compiler_params=pltpu.CompilerParams(
            collective_id=0, has_side_effects=True, vmem_limit_bytes=56 * 1024 * 1024
        ),
    )(
        queries,
        forget_logits,
        values,
        gate_input,
        states,
        gain.reshape(1, -1),
        weight,
        dealing,
        accepted,
    )


def solution(mesh):
    placed = (
        P("req", None, "head"),
        P("req", None, "head"),
        P("req", None, "head"),
        P("req", None, "head"),
        P("req", "head", None, None),
        P(),
        P("head", None),
        P("req"),
        P("req"),
    )
    return jax.shard_map(
        functools.partial(per_device, mesh.shape["req"], mesh.shape["head"]),
        mesh=mesh,
        in_specs=placed,
        out_specs=(P("req", None, "head"), P("req", "head", None, None)),
        check_vma=False,
    )
```

```python
import functools

import jax
import jax.numpy as jnp
from jax import lax
from jax.experimental import pallas as pl
from jax.experimental.pallas import tpu as pltpu
from jax.sharding import PartitionSpec as P

lower_bound = 0.8
norm_eps = 1e-05
MESH = pl.DeviceIdType.MESH
CHUNKS = 4


def split(x):
    high = x.astype(jnp.bfloat16)
    return high, (x - high.astype(jnp.float32)).astype(jnp.bfloat16)


def mm(a, b, dims=((1,), (0,))):
    return lax.dot_general(a, b, (dims, ((), ())), preferred_element_type=jnp.float32)


def running_product(x):
    rows = lax.broadcasted_iota(jnp.int32, x.shape, 0)
    step = 1
    while step < x.shape[0]:
        x = x * jnp.where(rows >= step, pltpu.roll(x, step, 0), 1.0)
        step *= 2
    return x


def kernel(
    n_req,
    n_head,
    inner,
    direct,
    order,
    q_hbm,
    f_hbm,
    v_hbm,
    g_hbm,
    s_hbm,
    gain_hbm,
    w_hbm,
    dealing,
    accepted,
    out_ref,
    new_ref,
    raw,
    gath,
    chosen,
    deals,
    cross_out,
    cross_in,
    own,
    states,
    states_high,
    states_low,
    weight,
    gain,
    keys,
    decay,
    total,
    part_out,
    part_in,
    load_sem,
    small_sem,
    deal_send,
    deal_recv,
    line_send,
    line_recv,
    cross_send,
    cross_recv,
    part_send,
    part_recv,
):
    outer = n_req // inner
    chunks, _, draft, width = raw.shape
    heads, size = states.shape[0], states.shape[2]
    per = heads // chunks
    columns = out_ref.shape[2]
    me = lax.axis_index("req")
    mine = lax.axis_index("head")
    place = me // inner
    lane = lax.rem(me, inner)
    across = place * inner + (inner - 1 - lane)
    line = [(lax.rem(place + k, outer), lax.rem(place + outer - k, outer)) for k in range(1, outer)]
    ring = [lax.rem(mine + k, n_head) for k in range(1, n_head)]

    def start(source, target, sem):
        copy = pltpu.make_async_copy(source, target, sem)
        copy.start()
        return copy

    loads = [None] * chunks
    for c in order:
        loads[c] = [
            start(ref.at[0, :, pl.ds(c * width, width)], raw.at[c, a], load_sem.at[c, a])
            for a, ref in enumerate((q_hbm, f_hbm, v_hbm, g_hbm))
        ]
    barrier = pltpu.get_barrier_semaphore()
    peers = [(to * inner + lane, mine) for to, _ in line]
    if inner > 1:
        peers.append((across, mine))
    peers += [(me, to) for to in ring]
    for peer in peers:
        pl.semaphore_signal(barrier, inc=1, device_id=peer, device_id_type=MESH)
    state_load = start(s_hbm.at[0], states, small_sem.at[0])
    weight_load = start(w_hbm, weight, small_sem.at[1])
    gain_load = start(gain_hbm, gain, small_sem.at[2])
    deals[place] = jnp.full(deals.shape[1:], dealing[0], jnp.int32)
    for c in order:
        for load in loads[c]:
            load.wait()
    pl.semaphore_wait(barrier, len(peers))

    def deal_copy(k, slot, to):
        return pltpu.make_async_remote_copy(
            src_ref=deals.at[place],
            dst_ref=deals.at[slot],
            send_sem=deal_send.at[k],
            recv_sem=deal_recv.at[slot],
            device_id=(to, mine),
            device_id_type=MESH,
        )

    def line_copy(k, c, slot, to):
        return pltpu.make_async_remote_copy(
            src_ref=raw.at[c] if c in direct else chosen.at[to, c],
            dst_ref=gath.at[slot, c],
            send_sem=line_send.at[k, c],
            recv_sem=line_recv.at[slot, c],
            device_id=(to * inner + lane, mine),
            device_id_type=MESH,
        )

    def cross_copy(c):
        return pltpu.make_async_remote_copy(
            src_ref=cross_out.at[c] if c in direct else raw.at[c],
            dst_ref=cross_in.at[c],
            send_sem=cross_send.at[c],
            recv_sem=cross_recv.at[c],
            device_id=(across, mine),
            device_id_type=MESH,
        )

    turned = [c for c in order if c not in direct]
    if inner > 1:
        deal_copy(outer - 1, outer, across).start()
    for k, (to, _) in enumerate(line):
        deal_copy(k, place, to * inner + lane).start()
    for c in turned:
        cross_copy(c).start()
    for c in direct:
        for k, (to, _) in enumerate(line):
            line_copy(k, c, place, to).start()

    def mask_of(slot, target):
        hit = jnp.where(deals[slot] == target, 1.0, 0.0)
        hit = jnp.concatenate([hit] * (draft // 8), axis=0).astype(jnp.bfloat16)
        return jnp.concatenate([hit] * (width // 128), axis=1)

    if turned:
        deal_copy(outer - 1, outer, across).wait_recv()
        first = [mask_of(place, slot * inner + lane) for slot in range(outer)]
        second = [mask_of(outer, slot * inner + lane) for slot in range(outer)]
        for c in turned:
            cross_copy(c).wait_recv()
            for slot in range(outer):
                for a in range(4):
                    chosen[slot, c, a] = first[slot] * raw[c, a] + second[slot] * cross_in[c, a]
            for k, (to, _) in enumerate(line):
                line_copy(k, c, place, to).start()

    state_load.wait()
    for h in range(heads):
        states_high[h], states_low[h] = split(states[h])

    for k, (to, source) in enumerate(line):
        deal_copy(k, source, to * inner + lane).wait_recv()

    def pick(target, c):
        masks = [mask_of(lax.rem(place + k, outer), target) for k in range(outer)]
        for a in range(4):
            acc = masks[0] * raw[c, a]
            for k in range(1, outer):
                acc = acc + masks[k] * gath[lax.rem(place + k, outer), c, a]
            yield a, acc

    def collect(c):
        for k, (to, source) in enumerate(line):
            line_copy(k, c, source, to).wait_recv()

    for c in direct:
        collect(c)
        if inner > 1:
            for a, tokens in pick(across, c):
                cross_out[c, a] = tokens
            cross_copy(c).start()
        for a, tokens in pick(me, c):
            own[c, a] = tokens

    def tokens_of(c):
        if c in direct:
            if inner == 1:
                return [own[c, a] for a in range(4)]
            cross_copy(c).wait_recv()
            return [own[c, a] + cross_in[c, a] for a in range(4)]
        collect(c)
        found = []
        for a in range(4):
            acc = chosen[place, c, a]
            for k in range(1, outer):
                acc = acc + gath[lax.rem(place + k, outer), c, a]
            found.append(acc)
        return found

    row = lax.broadcasted_iota(jnp.int32, (draft, draft), 0)
    column = lax.broadcasted_iota(jnp.int32, (draft, draft), 1)
    causal = row >= column

    def mix(c):
        q, f, v, g = tokens_of(c)
        own[c, 2] = v
        forget = lower_bound + (1.0 - lower_bound) * jax.nn.sigmoid(f.astype(jnp.float32))
        products = running_product(forget)
        scaled = q.astype(jnp.float32) * products
        key = (1.0 - forget) / products
        decay[c] = products
        keys[c] = key
        gate = g.astype(jnp.float32)
        gate = gate * jax.nn.sigmoid(gate)
        q_high, q_low = split(scaled)
        k_high, k_low = split(key)
        results = []
        for i in range(per):
            h = c * per + i
            s = slice(i * size, (i + 1) * size)
            qh, ql = q_high[:, s], q_low[:, s]
            kh, kl = k_high[:, s], k_low[:, s]
            both = jnp.concatenate([qh, ql], axis=0)
            nt = ((1,), (1,))
            scores = mm(both, kh, nt)
            scores = scores[:draft] + scores[draft:] + mm(qh, kl, nt)
            scores = jnp.where(causal, scores, 0.0)
            a_high, a_low = split(scores)
            carried = mm(both, states_high[h])
            carried = carried[:draft] + carried[draft:] + mm(qh, states_low[h])
            local = mm(jnp.concatenate([a_high, a_low], axis=0), v[:, s])
            o = carried + local[:draft] + local[draft:]
            meansq = jnp.mean(o * o, axis=-1, keepdims=True)
            results.append(o * lax.rsqrt(meansq + norm_eps) * gain[...] * gate[:, s])
        return jnp.concatenate(results, axis=1).astype(jnp.bfloat16)

    def project(c, mixed):
        rows = pl.ds(c * width, width)
        for j in range(n_head):
            part = mm(mixed, weight[rows, j * columns : (j + 1) * columns])
            if c != order[0]:
                part = part + total[j]
            total[j] = part
            if c == order[-1]:
                part_out[j] = part.astype(jnp.bfloat16)

    def advance(c):
        taken = accepted[0]
        rows = lax.broadcasted_iota(jnp.int32, (draft, width), 0)
        last = jnp.sum(jnp.where(rows == taken - 1, decay[c], 0.0), axis=0, keepdims=True)
        last = jnp.where(taken == 0, 1.0, last)
        key = jnp.where(rows < taken, keys[c] * last, 0.0)
        k_high, k_low = split(key)
        both = jnp.concatenate([k_high, k_low], axis=0)
        v = own[c, 2]
        twice = jnp.concatenate([v, v], axis=0)
        for i in range(per):
            h = c * per + i
            s = slice(i * size, (i + 1) * size)
            fade = jnp.broadcast_to(last[:, s], (size, size)).T
            new_ref[0, h] = fade * states[h] + mm(both[:, s], twice[:, s], ((0,), (0,)))

    def part_copy(k, slot, to):
        return pltpu.make_async_remote_copy(
            src_ref=part_out.at[to],
            dst_ref=part_in.at[slot],
            send_sem=part_send.at[k],
            recv_sem=part_recv.at[slot],
            device_id=(me, to),
            device_id_type=MESH,
        )

    gain_load.wait()
    weight_load.wait()
    for c in order:
        project(c, mix(c))
    for k, to in enumerate(ring):
        part_copy(k, mine, to).start()
    for c in order:
        advance(c)
    result = total[mine]
    for k in range(n_head - 1):
        source = lax.rem(mine + n_head - 1 - k, n_head)
        part_copy(k, source, ring[k]).wait_recv()
        result = result + part_in[source].astype(jnp.float32)
    out_ref[0] = result.astype(jnp.bfloat16)

    if inner > 1:
        deal_copy(outer - 1, outer, across).wait_send()
    for k, (to, _) in enumerate(line):
        deal_copy(k, place, to * inner + lane).wait_send()
        for c in range(chunks):
            line_copy(k, c, place, to).wait_send()
    if inner > 1:
        for c in range(chunks):
            cross_copy(c).wait_send()
    for k, to in enumerate(ring):
        part_copy(k, mine, to).wait_send()


def per_device(n_req, n_head, *args):
    queries, forget_logits, values, gate_input, states, gain, weight, dealing, accepted = args
    draft, features = queries.shape[1:]
    heads, size = states.shape[1:3]
    columns = weight.shape[1] // n_head
    inner = 2 if n_req % 2 == 0 else 1
    outer = n_req // inner
    chunks = CHUNKS if heads % CHUNKS == 0 else 1
    direct = (0,) if inner > 1 else tuple(range(chunks))
    order = (1, 0, 2, 3) if chunks == 4 else tuple(range(chunks))
    width = features // chunks
    bf16, f32 = jnp.bfloat16, jnp.float32
    hbm = pl.BlockSpec(memory_space=pltpu.HBM)
    vmem = pl.BlockSpec(memory_space=pltpu.VMEM)
    smem = pl.BlockSpec(memory_space=pltpu.SMEM)
    dma = pltpu.SemaphoreType.DMA
    return pl.pallas_call(
        functools.partial(kernel, n_req, n_head, inner, direct, order),
        out_shape=(
            jax.ShapeDtypeStruct((1, draft, columns), bf16),
            jax.ShapeDtypeStruct(states.shape, f32),
        ),
        in_specs=[hbm] * 7 + [smem] * 2,
        out_specs=(vmem, vmem),
        scratch_shapes=[
            pltpu.VMEM((chunks, 4, draft, width), bf16),
            pltpu.VMEM((outer, chunks, 4, draft, width), bf16),
            pltpu.VMEM((outer, chunks, 4, draft, width), bf16),
            pltpu.VMEM((outer + 1, 8, 128), jnp.int32),
            pltpu.VMEM((chunks, 4, draft, width), bf16),
            pltpu.VMEM((chunks, 4, draft, width), bf16),
            pltpu.VMEM((chunks, 4, draft, width), bf16),
            pltpu.VMEM((heads, size, size), f32),
            pltpu.VMEM((heads, size, size), bf16),
            pltpu.VMEM((heads, size, size), bf16),
            pltpu.VMEM(weight.shape, bf16),
            pltpu.VMEM((1, size), f32),
            pltpu.VMEM((chunks, draft, width), f32),
            pltpu.VMEM((chunks, draft, width), f32),
            pltpu.VMEM((n_head, draft, columns), f32),
            pltpu.VMEM((n_head, draft, columns), bf16),
            pltpu.VMEM((n_head, draft, columns), bf16),
            dma((chunks, 4)),
            dma((3,)),
            dma((outer,)),
            dma((outer + 1,)),
            dma((outer, chunks)),
            dma((outer, chunks)),
            dma((chunks,)),
            dma((chunks,)),
            dma((n_head,)),
            dma((n_head,)),
        ],
        compiler_params=pltpu.CompilerParams(
            collective_id=0, has_side_effects=True, vmem_limit_bytes=24 * 1024 * 1024
        ),
    )(
        *[
            pltpu.with_memory_space_constraint(x, pltpu.HBM)
            for x in (queries, forget_logits, values, gate_input, states, gain.reshape(1, -1), weight)
        ],
        dealing,
        accepted,
    )


def solution(mesh):
    placed = (
        P("req", None, "head"),
        P("req", None, "head"),
        P("req", None, "head"),
        P("req", None, "head"),
        P("req", "head", None, None),
        P(),
        P("head", None),
        P("req"),
        P("req"),
    )
    return jax.shard_map(
        functools.partial(per_device, mesh.shape["req"], mesh.shape["head"]),
        mesh=mesh,
        in_specs=placed,
        out_specs=(P("req", None, "head"), P("req", "head", None, None)),
        check_vma=False,
    )
```

```python
import functools

import jax
import jax.numpy as jnp
from jax import lax
from jax.experimental import pallas as pl
from jax.experimental.pallas import tpu as pltpu
from jax.sharding import PartitionSpec as P

lower_bound = 0.8
norm_eps = 1e-05
MESH = pl.DeviceIdType.MESH
CHUNKS = 4


def split(x):
    high = x.astype(jnp.bfloat16)
    return high, (x - high.astype(jnp.float32)).astype(jnp.bfloat16)


def mm(a, b, dims=((1,), (0,))):
    return lax.dot_general(a, b, (dims, ((), ())), preferred_element_type=jnp.float32)


def running_product(x):
    rows = lax.broadcasted_iota(jnp.int32, x.shape, 0)
    step = 1
    while step < x.shape[0]:
        x = x * jnp.where(rows >= step, pltpu.roll(x, step, 0), 1.0)
        step *= 2
    return x


def kernel(
    n_req,
    n_head,
    inner,
    direct,
    order,
    q_hbm,
    f_hbm,
    v_hbm,
    g_hbm,
    s_hbm,
    gain_hbm,
    w_hbm,
    dealing,
    accepted,
    out_ref,
    new_ref,
    raw,
    gath,
    chosen,
    deals,
    cross_out,
    cross_in,
    own,
    states,
    states_high,
    states_low,
    weight,
    gain,
    keys,
    decay,
    total,
    part_out,
    part_in,
    load_sem,
    small_sem,
    deal_send,
    deal_recv,
    line_send,
    line_recv,
    cross_send,
    cross_recv,
    part_send,
    part_recv,
):
    outer = n_req // inner
    chunks, _, draft, width = raw.shape
    heads, size = states.shape[0], states.shape[2]
    per = heads // chunks
    columns = out_ref.shape[2]
    me = lax.axis_index("req")
    mine = lax.axis_index("head")
    place = me // inner
    lane = lax.rem(me, inner)
    across = place * inner + (inner - 1 - lane)
    line = [(lax.rem(place + k, outer), lax.rem(place + outer - k, outer)) for k in range(1, outer)]
    ring = [lax.rem(mine + k, n_head) for k in range(1, n_head)]

    def start(source, target, sem):
        copy = pltpu.make_async_copy(source, target, sem)
        copy.start()
        return copy

    loads = [None] * chunks
    for c in order:
        loads[c] = [
            start(ref.at[0, :, pl.ds(c * width, width)], raw.at[c, a], load_sem.at[c, a])
            for a, ref in enumerate((q_hbm, f_hbm, v_hbm, g_hbm))
        ]
    barrier = pltpu.get_barrier_semaphore()
    peers = [(to * inner + lane, mine) for to, _ in line]
    if inner > 1:
        peers.append((across, mine))
    peers += [(me, to) for to in ring]
    for peer in peers:
        pl.semaphore_signal(barrier, inc=1, device_id=peer, device_id_type=MESH)
    state_load = start(s_hbm.at[0], states, small_sem.at[0])
    weight_load = start(w_hbm, weight, small_sem.at[1])
    gain_load = start(gain_hbm, gain, small_sem.at[2])
    deals[place] = jnp.full(deals.shape[1:], dealing[0], jnp.int32)
    for c in order:
        for load in loads[c]:
            load.wait()
    pl.semaphore_wait(barrier, len(peers))

    def deal_copy(k, slot, to):
        return pltpu.make_async_remote_copy(
            src_ref=deals.at[place],
            dst_ref=deals.at[slot],
            send_sem=deal_send.at[k],
            recv_sem=deal_recv.at[slot],
            device_id=(to, mine),
            device_id_type=MESH,
        )

    def line_copy(k, c, slot, to):
        return pltpu.make_async_remote_copy(
            src_ref=raw.at[c] if c in direct else chosen.at[to, c],
            dst_ref=gath.at[slot, c],
            send_sem=line_send.at[k, c],
            recv_sem=line_recv.at[slot, c],
            device_id=(to * inner + lane, mine),
            device_id_type=MESH,
        )

    def cross_copy(c):
        return pltpu.make_async_remote_copy(
            src_ref=cross_out.at[c] if c in direct else raw.at[c],
            dst_ref=cross_in.at[c],
            send_sem=cross_send.at[c],
            recv_sem=cross_recv.at[c],
            device_id=(across, mine),
            device_id_type=MESH,
        )

    turned = [c for c in order if c not in direct]
    if inner > 1:
        deal_copy(outer - 1, outer, across).start()
    for k, (to, _) in enumerate(line):
        deal_copy(k, place, to * inner + lane).start()
    for c in turned:
        cross_copy(c).start()
    for c in direct:
        for k, (to, _) in enumerate(line):
            line_copy(k, c, place, to).start()

    def mask_of(slot, target):
        hit = jnp.where(deals[slot] == target, 1.0, 0.0)
        hit = jnp.concatenate([hit] * (draft // 8), axis=0).astype(jnp.bfloat16)
        return jnp.concatenate([hit] * (width // 128), axis=1)

    if turned:
        deal_copy(outer - 1, outer, across).wait_recv()
        first = [mask_of(place, slot * inner + lane) for slot in range(outer)]
        second = [mask_of(outer, slot * inner + lane) for slot in range(outer)]
        for c in turned:
            cross_copy(c).wait_recv()
            for slot in range(outer):
                for a in range(4):
                    chosen[slot, c, a] = first[slot] * raw[c, a] + second[slot] * cross_in[c, a]
            for k, (to, _) in enumerate(line):
                line_copy(k, c, place, to).start()

    state_load.wait()
    for h in range(heads):
        states_high[h], states_low[h] = split(states[h])

    for k, (to, source) in enumerate(line):
        deal_copy(k, source, to * inner + lane).wait_recv()

    def pick(target, c):
        masks = [mask_of(lax.rem(place + k, outer), target) for k in range(outer)]
        for a in range(4):
            acc = masks[0] * raw[c, a]
            for k in range(1, outer):
                acc = acc + masks[k] * gath[lax.rem(place + k, outer), c, a]
            yield a, acc

    def collect(c):
        for k, (to, source) in enumerate(line):
            line_copy(k, c, source, to).wait_recv()

    for c in direct:
        collect(c)
        if inner > 1:
            for a, tokens in pick(across, c):
                cross_out[c, a] = tokens
            cross_copy(c).start()
        for a, tokens in pick(me, c):
            own[c, a] = tokens

    def tokens_of(c):
        if c in direct:
            if inner == 1:
                return [own[c, a] for a in range(4)]
            cross_copy(c).wait_recv()
            return [own[c, a] + cross_in[c, a] for a in range(4)]
        collect(c)
        found = []
        for a in range(4):
            acc = chosen[place, c, a]
            for k in range(1, outer):
                acc = acc + gath[lax.rem(place + k, outer), c, a]
            found.append(acc)
        return found

    row = lax.broadcasted_iota(jnp.int32, (draft, draft), 0)
    column = lax.broadcasted_iota(jnp.int32, (draft, draft), 1)
    causal = row >= column

    def mix(c):
        q, f, v, g = tokens_of(c)
        own[c, 2] = v
        forget = lower_bound + (1.0 - lower_bound) * jax.nn.sigmoid(f.astype(jnp.float32))
        products = running_product(forget)
        scaled = q.astype(jnp.float32) * products
        key = (1.0 - forget) / products
        decay[c] = products
        keys[c] = key
        gate = g.astype(jnp.float32)
        gate = gate * jax.nn.sigmoid(gate)
        q_high, q_low = split(scaled)
        k_high, k_low = split(key)
        results = []
        for i in range(per):
            h = c * per + i
            s = slice(i * size, (i + 1) * size)
            qh, ql = q_high[:, s], q_low[:, s]
            kh, kl = k_high[:, s], k_low[:, s]
            both = jnp.concatenate([qh, ql], axis=0)
            nt = ((1,), (1,))
            scores = mm(both, kh, nt)
            scores = scores[:draft] + scores[draft:] + mm(qh, kl, nt)
            scores = jnp.where(causal, scores, 0.0)
            a_high, a_low = split(scores)
            carried = mm(both, states_high[h])
            carried = carried[:draft] + carried[draft:] + mm(qh, states_low[h])
            local = mm(jnp.concatenate([a_high, a_low], axis=0), v[:, s])
            o = carried + local[:draft] + local[draft:]
            meansq = jnp.mean(o * o, axis=-1, keepdims=True)
            results.append(o * lax.rsqrt(meansq + norm_eps) * gain[...] * gate[:, s])
        return jnp.concatenate(results, axis=1).astype(jnp.bfloat16)

    def project(c, mixed):
        rows = pl.ds(c * width, width)
        for j in range(n_head):
            part = mm(mixed, weight[rows, j * columns : (j + 1) * columns])
            if c != order[0]:
                part = part + total[j]
            total[j] = part
            if c == order[-1]:
                part_out[j] = part.astype(jnp.bfloat16)

    def advance(c):
        taken = accepted[0]
        rows = lax.broadcasted_iota(jnp.int32, (draft, width), 0)
        last = jnp.sum(jnp.where(rows == taken - 1, decay[c], 0.0), axis=0, keepdims=True)
        last = jnp.where(taken == 0, 1.0, last)
        key = jnp.where(rows < taken, keys[c] * last, 0.0)
        k_high, k_low = split(key)
        both = jnp.concatenate([k_high, k_low], axis=0)
        v = own[c, 2]
        twice = jnp.concatenate([v, v], axis=0)
        for i in range(per):
            h = c * per + i
            s = slice(i * size, (i + 1) * size)
            fade = jnp.broadcast_to(last[:, s], (size, size)).T
            new_ref[0, h] = fade * states[h] + mm(both[:, s], twice[:, s], ((0,), (0,)))

    def part_copy(k, slot, to):
        return pltpu.make_async_remote_copy(
            src_ref=part_out.at[to],
            dst_ref=part_in.at[slot],
            send_sem=part_send.at[k],
            recv_sem=part_recv.at[slot],
            device_id=(me, to),
            device_id_type=MESH,
        )

    gain_load.wait()
    weight_load.wait()
    for c in order:
        project(c, mix(c))
    for k, to in enumerate(ring):
        part_copy(k, mine, to).start()
    for c in order:
        advance(c)
    result = total[mine]
    for k in range(n_head - 1):
        source = lax.rem(mine + n_head - 1 - k, n_head)
        part_copy(k, source, ring[k]).wait_recv()
        result = result + part_in[source].astype(jnp.float32)
    out_ref[0] = result.astype(jnp.bfloat16)

    if inner > 1:
        deal_copy(outer - 1, outer, across).wait_send()
    for k, (to, _) in enumerate(line):
        deal_copy(k, place, to * inner + lane).wait_send()
        for c in range(chunks):
            line_copy(k, c, place, to).wait_send()
    if inner > 1:
        for c in range(chunks):
            cross_copy(c).wait_send()
    for k, to in enumerate(ring):
        part_copy(k, mine, to).wait_send()


def per_device(n_req, n_head, *args):
    queries, forget_logits, values, gate_input, states, gain, weight, dealing, accepted = args
    draft, features = queries.shape[1:]
    heads, size = states.shape[1:3]
    columns = weight.shape[1] // n_head
    inner = 2 if n_req % 2 == 0 else 1
    outer = n_req // inner
    chunks = CHUNKS if heads % CHUNKS == 0 else 1
    direct = tuple(range(max(1, chunks // 2))) if inner > 1 else tuple(range(chunks))
    order = (0, 2, 1, 3) if chunks == 4 else tuple(range(chunks))
    width = features // chunks
    bf16, f32 = jnp.bfloat16, jnp.float32
    hbm = pl.BlockSpec(memory_space=pltpu.HBM)
    vmem = pl.BlockSpec(memory_space=pltpu.VMEM)
    smem = pl.BlockSpec(memory_space=pltpu.SMEM)
    dma = pltpu.SemaphoreType.DMA
    return pl.pallas_call(
        functools.partial(kernel, n_req, n_head, inner, direct, order),
        out_shape=(
            jax.ShapeDtypeStruct((1, draft, columns), bf16),
            jax.ShapeDtypeStruct(states.shape, f32),
        ),
        in_specs=[hbm] * 7 + [smem] * 2,
        out_specs=(vmem, vmem),
        scratch_shapes=[
            pltpu.VMEM((chunks, 4, draft, width), bf16),
            pltpu.VMEM((outer, chunks, 4, draft, width), bf16),
            pltpu.VMEM((outer, chunks, 4, draft, width), bf16),
            pltpu.VMEM((outer + 1, 8, 128), jnp.int32),
            pltpu.VMEM((chunks, 4, draft, width), bf16),
            pltpu.VMEM((chunks, 4, draft, width), bf16),
            pltpu.VMEM((chunks, 4, draft, width), bf16),
            pltpu.VMEM((heads, size, size), f32),
            pltpu.VMEM((heads, size, size), bf16),
            pltpu.VMEM((heads, size, size), bf16),
            pltpu.VMEM(weight.shape, bf16),
            pltpu.VMEM((1, size), f32),
            pltpu.VMEM((chunks, draft, width), f32),
            pltpu.VMEM((chunks, draft, width), f32),
            pltpu.VMEM((n_head, draft, columns), f32),
            pltpu.VMEM((n_head, draft, columns), bf16),
            pltpu.VMEM((n_head, draft, columns), bf16),
            dma((chunks, 4)),
            dma((3,)),
            dma((outer,)),
            dma((outer + 1,)),
            dma((outer, chunks)),
            dma((outer, chunks)),
            dma((chunks,)),
            dma((chunks,)),
            dma((n_head,)),
            dma((n_head,)),
        ],
        compiler_params=pltpu.CompilerParams(
            collective_id=0, has_side_effects=True, vmem_limit_bytes=24 * 1024 * 1024
        ),
    )(
        *[
            pltpu.with_memory_space_constraint(x, pltpu.HBM)
            for x in (queries, forget_logits, values, gate_input, states, gain.reshape(1, -1), weight)
        ],
        dealing,
        accepted,
    )


def solution(mesh):
    placed = (
        P("req", None, "head"),
        P("req", None, "head"),
        P("req", None, "head"),
        P("req", None, "head"),
        P("req", "head", None, None),
        P(),
        P("head", None),
        P("req"),
        P("req"),
    )
    return jax.shard_map(
        functools.partial(per_device, mesh.shape["req"], mesh.shape["head"]),
        mesh=mesh,
        in_specs=placed,
        out_specs=(P("req", None, "head"), P("req", "head", None, None)),
        check_vma=False,
    )
```

```python
import functools

import jax
import jax.numpy as jnp
from jax import lax
from jax.experimental import pallas as pl
from jax.experimental.pallas import tpu as pltpu
from jax.sharding import PartitionSpec as P

lower_bound = 0.8
norm_eps = 1e-05
MESH = pl.DeviceIdType.MESH
CHUNKS = 4


def split(x):
    high = x.astype(jnp.bfloat16)
    return high, (x - high.astype(jnp.float32)).astype(jnp.bfloat16)


def mm(a, b, dims=((1,), (0,))):
    return lax.dot_general(a, b, (dims, ((), ())), preferred_element_type=jnp.float32)


def running_product(x):
    rows = lax.broadcasted_iota(jnp.int32, x.shape, 0)
    step = 1
    while step < x.shape[0]:
        x = x * jnp.where(rows >= step, pltpu.roll(x, step, 0), 1.0)
        step *= 2
    return x


def kernel(
    n_req,
    n_head,
    inner,
    direct,
    order,
    q_hbm,
    f_hbm,
    v_hbm,
    g_hbm,
    s_hbm,
    gain_hbm,
    w_hbm,
    dealing,
    accepted,
    out_ref,
    new_ref,
    raw,
    gath,
    chosen,
    deals,
    cross_out,
    cross_in,
    own,
    states,
    states_high,
    states_low,
    weight,
    gain,
    keys,
    decay,
    total,
    part_out,
    part_in,
    load_sem,
    small_sem,
    deal_send,
    deal_recv,
    line_send,
    line_recv,
    cross_send,
    cross_recv,
    part_send,
    part_recv,
):
    outer = n_req // inner
    chunks, _, draft, width = raw.shape
    heads, size = states.shape[0], states.shape[2]
    per = heads // chunks
    columns = out_ref.shape[2]
    me = lax.axis_index("req")
    mine = lax.axis_index("head")
    place = me // inner
    lane = lax.rem(me, inner)
    across = place * inner + (inner - 1 - lane)
    line = [(lax.rem(place + k, outer), lax.rem(place + outer - k, outer)) for k in range(1, outer)]
    ring = [lax.rem(mine + k, n_head) for k in range(1, n_head)]

    def start(source, target, sem):
        copy = pltpu.make_async_copy(source, target, sem)
        copy.start()
        return copy

    loads = [None] * chunks
    for c in order:
        loads[c] = [
            start(ref.at[0, :, pl.ds(c * width, width)], raw.at[c, a], load_sem.at[c, a])
            for a, ref in enumerate((q_hbm, f_hbm, v_hbm, g_hbm))
        ]
    barrier = pltpu.get_barrier_semaphore()
    peers = [(to * inner + lane, mine) for to, _ in line]
    if inner > 1:
        peers.append((across, mine))
    peers += [(me, to) for to in ring]
    for peer in peers:
        pl.semaphore_signal(barrier, inc=1, device_id=peer, device_id_type=MESH)
    state_load = start(s_hbm.at[0], states, small_sem.at[0])
    weight_load = start(w_hbm, weight, small_sem.at[1])
    gain_load = start(gain_hbm, gain, small_sem.at[2])
    deals[place] = jnp.full(deals.shape[1:], dealing[0], jnp.int32)
    for c in order:
        for load in loads[c]:
            load.wait()
    pl.semaphore_wait(barrier, len(peers))

    def deal_copy(k, slot, to):
        return pltpu.make_async_remote_copy(
            src_ref=deals.at[place],
            dst_ref=deals.at[slot],
            send_sem=deal_send.at[k],
            recv_sem=deal_recv.at[slot],
            device_id=(to, mine),
            device_id_type=MESH,
        )

    def line_copy(k, c, slot, to):
        return pltpu.make_async_remote_copy(
            src_ref=raw.at[c] if c in direct else chosen.at[to, c],
            dst_ref=gath.at[slot, c],
            send_sem=line_send.at[k, c],
            recv_sem=line_recv.at[slot, c],
            device_id=(to * inner + lane, mine),
            device_id_type=MESH,
        )

    def cross_copy(c):
        return pltpu.make_async_remote_copy(
            src_ref=cross_out.at[c] if c in direct else raw.at[c],
            dst_ref=cross_in.at[c],
            send_sem=cross_send.at[c],
            recv_sem=cross_recv.at[c],
            device_id=(across, mine),
            device_id_type=MESH,
        )

    turned = [c for c in order if c not in direct]
    if inner > 1:
        deal_copy(outer - 1, outer, across).start()
    if direct:
        for k, (to, _) in enumerate(line):
            deal_copy(k, place, to * inner + lane).start()
    for c in turned:
        cross_copy(c).start()
    for c in direct:
        for k, (to, _) in enumerate(line):
            line_copy(k, c, place, to).start()

    def mask_of(slot, target):
        hit = jnp.where(deals[slot] == target, 1.0, 0.0)
        hit = jnp.concatenate([hit] * (draft // 8), axis=0).astype(jnp.bfloat16)
        return jnp.concatenate([hit] * (width // 128), axis=1)

    if turned:
        deal_copy(outer - 1, outer, across).wait_recv()
        first = [mask_of(place, slot * inner + lane) for slot in range(outer)]
        second = [mask_of(outer, slot * inner + lane) for slot in range(outer)]
        for c in turned:
            cross_copy(c).wait_recv()
            for slot in range(outer):
                for a in range(4):
                    chosen[slot, c, a] = first[slot] * raw[c, a] + second[slot] * cross_in[c, a]
            for k, (to, _) in enumerate(line):
                line_copy(k, c, place, to).start()

    state_load.wait()
    for h in range(heads):
        states_high[h], states_low[h] = split(states[h])

    if direct:
        for k, (to, source) in enumerate(line):
            deal_copy(k, source, to * inner + lane).wait_recv()

    def pick(target, c):
        masks = [mask_of(lax.rem(place + k, outer), target) for k in range(outer)]
        for a in range(4):
            acc = masks[0] * raw[c, a]
            for k in range(1, outer):
                acc = acc + masks[k] * gath[lax.rem(place + k, outer), c, a]
            yield a, acc

    def collect(c):
        for k, (to, source) in enumerate(line):
            line_copy(k, c, source, to).wait_recv()

    for c in direct:
        collect(c)
        if inner > 1:
            for a, tokens in pick(across, c):
                cross_out[c, a] = tokens
            cross_copy(c).start()
        for a, tokens in pick(me, c):
            own[c, a] = tokens

    def tokens_of(c):
        if c in direct:
            if inner == 1:
                return [own[c, a] for a in range(4)]
            cross_copy(c).wait_recv()
            return [own[c, a] + cross_in[c, a] for a in range(4)]
        collect(c)
        found = []
        for a in range(4):
            acc = chosen[place, c, a]
            for k in range(1, outer):
                acc = acc + gath[lax.rem(place + k, outer), c, a]
            found.append(acc)
        return found

    row = lax.broadcasted_iota(jnp.int32, (draft, draft), 0)
    column = lax.broadcasted_iota(jnp.int32, (draft, draft), 1)
    causal = row >= column

    def mix(c):
        q, f, v, g = tokens_of(c)
        own[c, 2] = v
        forget = lower_bound + (1.0 - lower_bound) * jax.nn.sigmoid(f.astype(jnp.float32))
        products = running_product(forget)
        scaled = q.astype(jnp.float32) * products
        key = (1.0 - forget) / products
        decay[c] = products
        keys[c] = key
        gate = g.astype(jnp.float32)
        gate = gate * jax.nn.sigmoid(gate)
        q_high, q_low = split(scaled)
        k_high, k_low = split(key)
        results = []
        for i in range(per):
            h = c * per + i
            s = slice(i * size, (i + 1) * size)
            qh, ql = q_high[:, s], q_low[:, s]
            kh, kl = k_high[:, s], k_low[:, s]
            both = jnp.concatenate([qh, ql], axis=0)
            nt = ((1,), (1,))
            scores = mm(both, kh, nt)
            scores = scores[:draft] + scores[draft:] + mm(qh, kl, nt)
            scores = jnp.where(causal, scores, 0.0)
            a_high, a_low = split(scores)
            carried = mm(both, states_high[h])
            carried = carried[:draft] + carried[draft:] + mm(qh, states_low[h])
            local = mm(jnp.concatenate([a_high, a_low], axis=0), v[:, s])
            o = carried + local[:draft] + local[draft:]
            meansq = jnp.mean(o * o, axis=-1, keepdims=True)
            results.append(o * lax.rsqrt(meansq + norm_eps) * gain[...] * gate[:, s])
        return jnp.concatenate(results, axis=1).astype(jnp.bfloat16)

    def project(c, mixed):
        rows = pl.ds(c * width, width)
        for j in range(n_head):
            part = mm(mixed, weight[rows, j * columns : (j + 1) * columns])
            if c != order[0]:
                part = part + total[j]
            total[j] = part
            if c == order[-1]:
                part_out[j] = part.astype(jnp.bfloat16)

    def advance(c):
        taken = accepted[0]
        rows = lax.broadcasted_iota(jnp.int32, (draft, width), 0)
        last = jnp.sum(jnp.where(rows == taken - 1, decay[c], 0.0), axis=0, keepdims=True)
        last = jnp.where(taken == 0, 1.0, last)
        key = jnp.where(rows < taken, keys[c] * last, 0.0)
        k_high, k_low = split(key)
        both = jnp.concatenate([k_high, k_low], axis=0)
        v = own[c, 2]
        twice = jnp.concatenate([v, v], axis=0)
        for i in range(per):
            h = c * per + i
            s = slice(i * size, (i + 1) * size)
            fade = jnp.broadcast_to(last[:, s], (size, size)).T
            new_ref[0, h] = fade * states[h] + mm(both[:, s], twice[:, s], ((0,), (0,)))

    def part_copy(k, slot, to):
        return pltpu.make_async_remote_copy(
            src_ref=part_out.at[to],
            dst_ref=part_in.at[slot],
            send_sem=part_send.at[k],
            recv_sem=part_recv.at[slot],
            device_id=(me, to),
            device_id_type=MESH,
        )

    gain_load.wait()
    weight_load.wait()
    for c in order:
        project(c, mix(c))
    for k, to in enumerate(ring):
        part_copy(k, mine, to).start()
    for c in order:
        advance(c)
    result = total[mine]
    for k in range(n_head - 1):
        source = lax.rem(mine + n_head - 1 - k, n_head)
        part_copy(k, source, ring[k]).wait_recv()
        result = result + part_in[source].astype(jnp.float32)
    out_ref[0] = result.astype(jnp.bfloat16)

    if inner > 1:
        deal_copy(outer - 1, outer, across).wait_send()
    for k, (to, _) in enumerate(line):
        if direct:
            deal_copy(k, place, to * inner + lane).wait_send()
        for c in range(chunks):
            line_copy(k, c, place, to).wait_send()
    if inner > 1:
        for c in range(chunks):
            cross_copy(c).wait_send()
    for k, to in enumerate(ring):
        part_copy(k, mine, to).wait_send()


def per_device(n_req, n_head, *args):
    queries, forget_logits, values, gate_input, states, gain, weight, dealing, accepted = args
    draft, features = queries.shape[1:]
    heads, size = states.shape[1:3]
    columns = weight.shape[1] // n_head
    inner = 2 if n_req % 2 == 0 else 1
    outer = n_req // inner
    chunks = CHUNKS if heads % CHUNKS == 0 else 1
    direct = () if inner > 1 else tuple(range(chunks))
    order = tuple(range(chunks))
    width = features // chunks
    bf16, f32 = jnp.bfloat16, jnp.float32
    hbm = pl.BlockSpec(memory_space=pltpu.HBM)
    vmem = pl.BlockSpec(memory_space=pltpu.VMEM)
    smem = pl.BlockSpec(memory_space=pltpu.SMEM)
    dma = pltpu.SemaphoreType.DMA
    return pl.pallas_call(
        functools.partial(kernel, n_req, n_head, inner, direct, order),
        out_shape=(
            jax.ShapeDtypeStruct((1, draft, columns), bf16),
            jax.ShapeDtypeStruct(states.shape, f32),
        ),
        in_specs=[hbm] * 7 + [smem] * 2,
        out_specs=(vmem, vmem),
        scratch_shapes=[
            pltpu.VMEM((chunks, 4, draft, width), bf16),
            pltpu.VMEM((outer, chunks, 4, draft, width), bf16),
            pltpu.VMEM((outer, chunks, 4, draft, width), bf16),
            pltpu.VMEM((outer + 1, 8, 128), jnp.int32),
            pltpu.VMEM((chunks, 4, draft, width), bf16),
            pltpu.VMEM((chunks, 4, draft, width), bf16),
            pltpu.VMEM((chunks, 4, draft, width), bf16),
            pltpu.VMEM((heads, size, size), f32),
            pltpu.VMEM((heads, size, size), bf16),
            pltpu.VMEM((heads, size, size), bf16),
            pltpu.VMEM(weight.shape, bf16),
            pltpu.VMEM((1, size), f32),
            pltpu.VMEM((chunks, draft, width), f32),
            pltpu.VMEM((chunks, draft, width), f32),
            pltpu.VMEM((n_head, draft, columns), f32),
            pltpu.VMEM((n_head, draft, columns), bf16),
            pltpu.VMEM((n_head, draft, columns), bf16),
            dma((chunks, 4)),
            dma((3,)),
            dma((outer,)),
            dma((outer + 1,)),
            dma((outer, chunks)),
            dma((outer, chunks)),
            dma((chunks,)),
            dma((chunks,)),
            dma((n_head,)),
            dma((n_head,)),
        ],
        compiler_params=pltpu.CompilerParams(
            collective_id=0, has_side_effects=True, vmem_limit_bytes=24 * 1024 * 1024
        ),
    )(
        *[
            pltpu.with_memory_space_constraint(x, pltpu.HBM)
            for x in (queries, forget_logits, values, gate_input, states, gain.reshape(1, -1), weight)
        ],
        dealing,
        accepted,
    )


def solution(mesh):
    placed = (
        P("req", None, "head"),
        P("req", None, "head"),
        P("req", None, "head"),
        P("req", None, "head"),
        P("req", "head", None, None),
        P(),
        P("head", None),
        P("req"),
        P("req"),
    )
    return jax.shard_map(
        functools.partial(per_device, mesh.shape["req"], mesh.shape["head"]),
        mesh=mesh,
        in_specs=placed,
        out_specs=(P("req", None, "head"), P("req", "head", None, None)),
        check_vma=False,
    )
```
